1024 devices in a mesh: graph: 64 (over z, core), replica: 16 (over x, y).
Axes of the slice: x: 4, y: 4, z: 32, core: 2. Of those that a mesh axis runs over, the one named last changes fastest.
Arguments:
- features: bfloat16 [16, 8192, 512], P('replica', 'graph'), may hold values from -8 to 8
- neighbours: int32 [16, 8192, 16], P('replica', 'graph'), may hold values from 0 to 255
- send_rows: int32 [16, 64, 64, 2], P('replica', 'graph'), may hold values from 0 to 127
- send_counts: int32 [16, 64, 64], P('replica', 'graph'), may hold values from 0 to 2, as said below
- candidates: int32 [16, 2048, 512], P('replica', 'graph'), may hold values from 0 to 127
- perturbation: float32 [16, 2048, 4, 512], P('replica', 'graph'), may hold values from -320 to 320
- weight: bfloat16 [512, 512], replicated, may hold values from -0.25 to 0.25
Outputs:
- d_features: bfloat16 [16, 8192, 512], P('replica', 'graph')
- weight_grad: float32 [512, 512], P('graph', 'replica')
The draws below stay inside these ranges and needn't reach their ends.
Inputs may be any that keep to these rules, and one draw needn't show every extreme that they name: `send_counts`: rows that one device sends to another in its mini-batch; in every draw one device of each mini-batch receives 2 rows from every device.
All inputs are finite; a program needn't handle non-finite values.
Results may differ from the reference program's by a relative error of at most 0.013.
Values may be sent and summed in bfloat16 or wider, within the bound.
A program may use at most 32 MiB of HBM per device.

```python
import math
import jax
import jax.numpy as jnp
from jax import lax

D = 512
NODE_DEV = 128
CAP = 2
FANOUT = 16
CANDS = 512
TOP = 20
SAMPLES = 4
QUERY_DEV = 32
NODES = 8192
QUERIES = 2048
N_GRAPH = 64
N_REPLICA = 16


def draw_features(key, part):
    key = jax.random.fold_in(key, 11)
    first = jax.random.fold_in(key, 0)
    shape = (N_REPLICA, N_GRAPH * NODE_DEV, D)
    return jnp.clip(jax.random.normal(first, shape, jnp.float32), -6.0, 6.0).astype(jnp.bfloat16)


def draw_send_counts(key, part):
    key = jax.random.fold_in(key, 23)
    first, second, third = jax.random.split(key, 3)
    heat = jax.random.randint(first, (N_REPLICA, N_GRAPH, 1), 1, 5)
    ceiling = CAP * heat // 4
    counts = jax.random.randint(second, (N_REPLICA, N_GRAPH, N_GRAPH), 0, ceiling + 1)
    busiest = jax.random.randint(third, (N_REPLICA, 1, 1), 0, N_GRAPH)
    receiver = jnp.arange(N_GRAPH, dtype=jnp.int32)[None, :, None]
    return jnp.where(receiver == busiest, CAP, counts).astype(jnp.int32)


def draw_perturbation(key, part):
    key = jax.random.fold_in(key, 37)
    keys = jax.random.split(key, 1)
    shape = (N_REPLICA, N_GRAPH * QUERY_DEV, SAMPLES, CANDS)
    return jnp.clip(jax.random.normal(keys[0], shape, jnp.float32), -6.0, 6.0)


def set_ends(drawn, rng, smallest, high):
    longest = drawn.shape.index(max(drawn.shape))
    spots = []
    for shift in (0, 1):
        where = [jax.random.randint(jax.random.fold_in(rng, axis), (), 0, length) for axis, length in enumerate(drawn.shape)]
        where[longest] = (where[longest] + shift) % drawn.shape[longest]
        spots.append(tuple(where))
    return drawn.at[spots[0]].set(smallest).at[spots[1]].set(high)


def normal_values(rng, shape, width, limit, kind=jnp.bfloat16):
    return jnp.clip(width * jax.random.normal(rng, shape, jnp.float32), -limit, limit).astype(kind)


def setup_inputs(seed: int = 0) -> dict:
    seeds = jax.random.split(jax.random.key(seed), 8)
    return {
        "features": draw_features(jax.random.fold_in(seeds[7], 71), 0),
        "neighbours": set_ends(jax.random.randint(seeds[1], (N_REPLICA, NODES, FANOUT), 0, NODE_DEV + N_GRAPH * CAP), jax.random.fold_in(seeds[1], 1), 0, (NODE_DEV + N_GRAPH * CAP) - 1).astype(jnp.int32),
        "send_rows": set_ends(jax.random.randint(seeds[2], (N_REPLICA, N_GRAPH, N_GRAPH, CAP), 0, NODE_DEV), jax.random.fold_in(seeds[2], 1), 0, NODE_DEV - 1).astype(jnp.int32),
        "send_counts": draw_send_counts(jax.random.fold_in(seeds[7], 71), 0),
        "candidates": set_ends(jax.random.randint(seeds[4], (N_REPLICA, QUERIES, CANDS), 0, NODE_DEV), jax.random.fold_in(seeds[4], 1), 0, NODE_DEV - 1).astype(jnp.int32),
        "perturbation": draw_perturbation(jax.random.fold_in(seeds[7], 71), 0),
        "weight": normal_values(seeds[6], (D, D), D ** -0.5, 0.25),
    }


SCORE_SCALE = 16.0
LOSS_SCALE = 16.0
EPSILON = 1e-05

def embed_backward(mean_rows, weight, candidates, perturbation):
    query_count = candidates.shape[0]
    pre = jnp.dot(mean_rows, weight, preferred_element_type=jnp.float32)
    inverse = lax.rsqrt(lax.optimization_barrier(jnp.mean(pre * pre, axis=-1, keepdims=True)) + EPSILON)
    embedded = (pre * inverse).astype(jnp.bfloat16)
    similar = jnp.dot(embedded[:query_count], embedded.T, preferred_element_type=jnp.float32)
    factor = SCORE_SCALE / pre.shape[1]
    scores = factor * jnp.take_along_axis(similar, candidates, axis=1)
    perturbed = scores[:, None, :] + perturbation
    highest = lax.optimization_barrier(jnp.max(perturbed, axis=-1, keepdims=True))
    exponent = jnp.exp(perturbed - highest)
    weights_soft = exponent / lax.optimization_barrier(jnp.sum(exponent, axis=-1, keepdims=True))
    target = (jnp.arange(candidates.shape[1], dtype=jnp.int32) < TOP).astype(jnp.float32)
    d_scores = LOSS_SCALE * (TOP * lax.optimization_barrier(jnp.mean(weights_soft, axis=1)) - target[None, :])
    query_index = jnp.broadcast_to(jnp.arange(query_count, dtype=jnp.int32)[:, None], candidates.shape)
    d_similar = jnp.zeros((query_count, embedded.shape[0]), jnp.float32).at[query_index, candidates].add(d_scores).astype(jnp.bfloat16)
    d_embedded = factor * lax.dot_general(d_similar, embedded[:query_count], (((0,), (0,)), ((), ())), preferred_element_type=jnp.float32)
    d_queries = factor * jnp.dot(d_similar, embedded, preferred_element_type=jnp.float32)
    d_embedded = d_embedded.at[:query_count].add(d_queries)
    d_pre = inverse * d_embedded - inverse * inverse * inverse * pre * lax.optimization_barrier(jnp.mean(d_embedded * pre, axis=-1, keepdims=True))
    return d_pre.astype(jnp.bfloat16)

def device_pass(feature_rows, halo, keep, neighbour_rows, candidate_rows, noise_rows, weight):
    row_count = feature_rows.shape[0]
    table = jnp.concatenate([feature_rows, halo], axis=0)
    total = feature_rows.astype(jnp.float32) + lax.optimization_barrier(jnp.sum(table[neighbour_rows].astype(jnp.float32), axis=1))
    mean_rows = (total / (FANOUT + 1)).astype(jnp.bfloat16)
    d_pre = embed_backward(mean_rows, weight, candidate_rows, noise_rows)
    term = lax.dot_general(mean_rows, d_pre, (((0,), (0,)), ((), ())), preferred_element_type=jnp.float32)
    share = (jnp.dot(d_pre, weight.T, preferred_element_type=jnp.float32) / (FANOUT + 1)).astype(jnp.bfloat16)
    share_wide = share.astype(jnp.float32)
    spread = jnp.broadcast_to(share_wide[:, None, :], neighbour_rows.shape + (share.shape[1],))
    d_table = jnp.zeros(table.shape, jnp.float32).at[neighbour_rows].add(spread)
    d_local = share_wide + d_table[:row_count]
    halo_grad = jnp.where(keep[:, None], d_table[row_count:], 0.0).astype(jnp.bfloat16)
    return (d_local, halo_grad, term)

def reference(features, neighbours, send_rows, send_counts, candidates, perturbation, weight):
    feature_grid = features.reshape(N_REPLICA, N_GRAPH, NODE_DEV, D)
    neighbour_grid = neighbours.reshape(N_REPLICA, N_GRAPH, NODE_DEV, FANOUT)
    candidate_grid = candidates.reshape(N_REPLICA, N_GRAPH, QUERY_DEV, CANDS)
    noise_grid = perturbation.reshape(N_REPLICA, N_GRAPH, QUERY_DEV, SAMPLES, CANDS)
    source = jnp.arange(N_GRAPH, dtype=jnp.int32)[:, None]
    slots = jnp.arange(CAP, dtype=jnp.int32)[None, :]

    def replica_step(w_total, pieces):
        feature_rep, neighbour_rep, send_rep, count_rep, candidate_rep, noise_rep = pieces

        def device_step(w_sum, inner):
            position, neighbour_rows, candidate_rows, noise_rows, counts = inner
            rows_from = send_rep[:, position, :]
            keep = slots < counts[:, None]
            halo = jnp.where(keep[:, :, None], feature_rep[source, rows_from], jnp.zeros((), jnp.bfloat16))
            d_local, halo_grad, term = device_pass(feature_rep[position], halo.reshape(N_GRAPH * CAP, D), keep.reshape(-1), neighbour_rows, candidate_rows, noise_rows, weight)
            return (w_sum + term, (d_local, halo_grad))
        positions = jnp.arange(N_GRAPH, dtype=jnp.int32)
        w_total, (d_local, halo_grad) = lax.scan(device_step, w_total, (positions, neighbour_rep, candidate_rep, noise_rep, count_rep))
        returned = halo_grad.reshape(N_GRAPH, N_GRAPH, CAP, D).transpose(1, 0, 2, 3).astype(jnp.float32)
        d_rep = d_local.at[source[:, :, None], send_rep].add(returned)
        return (w_total, d_rep.astype(jnp.bfloat16))
    w_total, d_all = lax.scan(replica_step, jnp.zeros((D, D), jnp.float32), (feature_grid, neighbour_grid, send_rows, send_counts, candidate_grid, noise_grid))
    weight_grad = w_total / math.sqrt(N_GRAPH * N_REPLICA)
    return (d_all.reshape(N_REPLICA, NODES, D), weight_grad)
```

```python
import functools
import math

import jax
import jax.numpy as jnp
from jax import lax
from jax.experimental import pallas as pl
from jax.experimental.pallas import tpu as pltpu
from jax.sharding import PartitionSpec as P

TOP = 20
SCORE_SCALE = 16.0
LOSS_SCALE = 16.0
EPSILON = 1e-05
LANES = 128
MESH = pl.DeviceIdType.MESH
F32 = jnp.float32
BF16 = jnp.bfloat16


def iota(shape, axis):
    return lax.broadcasted_iota(jnp.int32, shape, axis)


def one_hot(mask):
    return jnp.where(mask, 1.0, 0.0).astype(BF16)


def dot(a, b, a_axis=1, b_axis=0):
    return lax.dot_general(
        a, b, (((a_axis,), (b_axis,)), ((), ())), preferred_element_type=F32
    )


def wait_all(ref, sem, count):
    part = ref.at[pl.ds(0, count)]
    pltpu.make_async_copy(part, part, sem).wait()


def kernel(
    groups,
    replicas,
    features,
    neighbours,
    send_rows,
    counts,
    candidates,
    perturbation,
    weight,
    d_features,
    weight_grad,
    stage,
    out_send,
    out_recv,
    ret_send,
    ret_recv,
    mean_send,
    mean_recv,
    dpre_send,
    dpre_recv,
    tile_send,
    tile_recv,
    z_send,
    z_recv,
    adj,
    adj_t,
    picks,
    noise,
    total,
    send_sems,
    recv_sems,
):
    mg = lax.axis_index("graph")
    mr = lax.axis_index("replica")
    core = lax.rem(mg, 2)
    chip = lax.div(mg, 2)
    chips = groups // 2
    partner = chip * 2 + 1 - core
    rows, width = features.shape
    fanout = neighbours.shape[0]
    capacity = send_rows.shape[0]
    queries, cands = candidates.shape
    samples = perturbation.shape[1]
    blocks = width // LANES
    parts = capacity * blocks
    slots = groups * capacity
    tall, wide = weight_grad.shape
    half = tall * chips

    barrier = pltpu.get_barrier_semaphore()

    def greet_graph(i, carry):
        pl.semaphore_signal(
            barrier, inc=1, device_id=(lax.rem(mg + i, groups), mr), device_id_type=MESH
        )
        return carry

    def greet_replica(i, carry):
        pl.semaphore_signal(
            barrier, inc=1, device_id=(mg, lax.rem(mr + i, replicas)), device_id_type=MESH
        )
        return carry

    lax.fori_loop(1, groups, greet_graph, 0)
    lax.fori_loop(1, replicas, greet_replica, 0)

    def far_first(i):
        step = lax.div(i + 1, 2)
        sign = 1 - 2 * lax.rem(i, 2)
        return lax.rem(mg + groups // 2 + sign * step + groups, groups)

    def send_all(source, target, slot):
        def step(i, carry):
            peer = far_first(i)
            pltpu.make_async_remote_copy(
                src_ref=source.at[peer],
                dst_ref=target.at[mg],
                send_sem=send_sems.at[slot],
                recv_sem=recv_sems.at[slot],
                device_id=(peer, mr),
                device_id_type=MESH,
            ).start()
            return carry

        lax.fori_loop(0, groups - 1, step, 0)

    def pack(values, target):
        for k in range(capacity):
            for j in range(blocks):
                stage[pl.ds(k * blocks + j, groups, stride=parts), :] = values[
                    k * groups : (k + 1) * groups, j * LANES : (j + 1) * LANES
                ]
        target[...] = stage[...].reshape(groups, parts, LANES).astype(BF16)

    def unpack(source):
        stage[...] = source[...].astype(F32).reshape(groups * parts, LANES)
        return jnp.concatenate(
            [
                jnp.concatenate(
                    [
                        stage[pl.ds(k * blocks + j, groups, stride=parts), :]
                        for j in range(blocks)
                    ],
                    axis=1,
                )
                for k in range(capacity)
            ],
            axis=0,
        ).astype(BF16)

    feature_rows = features[...]
    row_of = iota((rows, groups), 0)
    sent = [one_hot(row_of == send_rows[k : k + 1, :]) for k in range(capacity)]
    pack(
        jnp.concatenate([dot(s, feature_rows, 0, 0) for s in sent], axis=0), out_send
    )
    out_recv[mg] = out_send[mg]

    pl.semaphore_wait(barrier, groups + replicas - 2)
    send_all(out_send, out_recv, 0)

    table = rows + slots
    place = iota((table, rows), 0)
    past = place - rows
    slot_id = rows + capacity * lax.rem(past, groups) + lax.div(past, groups)
    name = jnp.where(past < 0, place, slot_id)
    counted = jnp.zeros((table, rows), F32)
    for f in range(fanout):
        counted = counted + jnp.where(neighbours[f : f + 1, :] == name, 1.0, 0.0)
    count_column = jnp.sum(
        jnp.where(iota((groups, groups), 0) == iota((groups, groups), 1), counts[...], 0),
        axis=1,
        keepdims=True,
    )
    keep = jnp.concatenate(
        [jnp.ones((rows, 1), F32)]
        + [jnp.where(count_column > k, 1.0, 0.0) for k in range(capacity)],
        axis=0,
    )
    counted = counted * keep
    adj_t[...] = counted.astype(BF16)
    adj[...] = counted.T.astype(BF16)
    node = iota((rows, cands), 0)

    def pick(q, carry):
        picks[pl.ds(pl.multiple_of(q * rows, rows), rows), :] = one_hot(
            candidates[pl.ds(q, 1), :] == node
        )
        return carry

    lax.fori_loop(0, queries, pick, 0)
    for m in range(samples):
        noise[m] = perturbation[:, m, :]
    total[...] = feature_rows.astype(F32) + dot(adj[:, :rows], feature_rows)
    column = iota((width, half), 0)
    order = iota((width, half), 1)
    wanted = (lax.rem(order, chips) * 2) * tall + lax.div(order, chips)
    mine = one_hot(column == wanted + core * tall)
    theirs = one_hot(column == wanted + (1 - core) * tall)

    wait_all(out_recv, recv_sems.at[0], groups - 1)
    halo = unpack(out_recv)
    scale = 1.0 / (fanout + 1)
    mean_rows = ((total[...] + dot(adj[:, rows:], halo)) * scale).astype(BF16)
    pre = dot(mean_rows, weight[...])
    inverse = lax.rsqrt(jnp.mean(pre * pre, axis=-1, keepdims=True) + EPSILON)
    embedded = (pre * inverse).astype(BF16)

    def to_partner(source, target, slot):
        return pltpu.make_async_remote_copy(
            src_ref=source,
            dst_ref=target,
            send_sem=send_sems.at[slot],
            recv_sem=recv_sems.at[slot],
            device_id=(partner, mr),
            device_id_type=MESH,
        )

    mean_send[...] = dot(mean_rows, theirs).astype(BF16)
    mean_copy = to_partner(mean_send, mean_recv, 1)
    mean_copy.start()
    mean_mine = dot(mean_rows, mine).astype(BF16)

    factor = SCORE_SCALE / width
    similar = factor * dot(embedded[:queries], embedded, 1, 1)
    scores = jnp.concatenate(
        [
            jnp.take_along_axis(
                similar,
                candidates[:, c * rows : (c + 1) * rows],
                axis=1,
                mode="promise_in_bounds",
            )
            for c in range(cands // rows)
        ],
        axis=1,
    )
    soft = jnp.zeros((queries, cands), F32)
    for m in range(samples):
        shifted = scores + noise[m]
        exponent = jnp.exp(shifted - jnp.max(shifted, axis=-1, keepdims=True))
        soft = soft + exponent * (1.0 / jnp.sum(exponent, axis=-1, keepdims=True))
    engaged = jnp.where(iota((queries, cands), 1) < TOP, LOSS_SCALE, 0.0)
    d_scores = (LOSS_SCALE * TOP / samples) * soft - engaged
    high = d_scores.astype(BF16)
    low = (d_scores - high.astype(F32)).astype(BF16)
    both = jnp.concatenate(
        [high, low, jnp.zeros((LANES - 2 * queries, cands), BF16)], axis=0
    )
    lane = iota((rows, LANES), 1)
    spread = jnp.zeros((rows, LANES), F32)
    group = 8
    for g in range(queries // group):
        some = dot(picks[g * group * rows : (g + 1) * group * rows, :], both, 1, 1)
        for i in range(group):
            q = g * group + i
            spread = spread + jnp.where(
                lax.rem(lane, queries) == q, some[i * rows : (i + 1) * rows, :], 0.0
            )
    spread = spread + pltpu.roll(spread, LANES - queries, axis=1)
    similar_t = jnp.where(lane < queries, spread, 0.0).astype(BF16).astype(F32)
    mixed = jnp.concatenate([similar_t, similar_t.T], axis=1).astype(BF16)
    d_embedded = factor * dot(mixed, jnp.concatenate([embedded, embedded], axis=0))
    slope = jnp.mean(d_embedded * pre, axis=-1, keepdims=True)
    d_pre = (inverse * d_embedded - inverse * inverse * inverse * pre * slope).astype(BF16)
    dpre_send[...] = d_pre
    dpre_copy = to_partner(dpre_send, dpre_recv, 2)
    dpre_copy.start()

    share = (dot(d_pre, weight[...], 1, 1) * scale).astype(BF16)
    pack(dot(adj_t[rows:, :], share), ret_send)
    ret_recv[mg] = ret_send[mg]
    send_all(ret_send, ret_recv, 3)
    total[...] = share.astype(F32) + dot(adj_t[:rows, :], share)

    mean_copy.wait()
    dpre_copy.wait()
    product = dot(d_pre, mean_mine, 0, 0) + dot(dpre_recv[...], mean_recv[...], 0, 0)
    tile_send[...] = product.astype(BF16).reshape(replicas, wide, half)
    tile_recv[mr] = tile_send[mr]

    def send_tile(i, carry):
        peer = lax.rem(mr + i, replicas)
        pltpu.make_async_remote_copy(
            src_ref=tile_send.at[peer],
            dst_ref=tile_recv.at[mr],
            send_sem=send_sems.at[4],
            recv_sem=recv_sems.at[4],
            device_id=(mg, peer),
            device_id_type=MESH,
        ).start()
        return carry

    lax.fori_loop(1, replicas, send_tile, 0)
    wait_all(tile_recv, recv_sems.at[4], replicas - 1)
    plane = tile_recv[0].astype(F32)
    for p in range(1, replicas):
        plane = plane + tile_recv[p].astype(F32)
    if wide < LANES:
        plane = jnp.concatenate([plane, jnp.zeros((LANES - wide, half), F32)], axis=0)
    plane_t = plane.T
    per = LANES // wide
    for h in range(tall // per):
        packed = plane_t[h * per * chips : (h * per + 1) * chips, :]
        for i in range(1, per):
            e = h * per + i
            packed = packed + pltpu.roll(
                plane_t[e * chips : (e + 1) * chips, :], i * wide, axis=1
            )
        for c in range(chips):
            z_send[c, h : h + 1, :] = packed[c : c + 1, :]
    z_recv[chip] = z_send[chip]

    def send_z(i, carry):
        peer = lax.rem(chip + i, chips)
        pltpu.make_async_remote_copy(
            src_ref=z_send.at[peer],
            dst_ref=z_recv.at[chip],
            send_sem=send_sems.at[5],
            recv_sem=recv_sems.at[5],
            device_id=(peer * 2 + core, mr),
            device_id_type=MESH,
        ).start()
        return carry

    lax.fori_loop(1, chips, send_z, 0)

    wait_all(ret_recv, recv_sems.at[3], groups - 1)
    returned = unpack(ret_recv)
    d_rows = total[...]
    for k in range(capacity):
        d_rows = d_rows + dot(sent[k], returned[k * groups : (k + 1) * groups, :])
    d_features[...] = d_rows.astype(BF16)

    wait_all(z_recv, recv_sems.at[5], chips - 1)
    block = jnp.sum(z_recv[...], axis=0) * (1.0 / math.sqrt(groups * replicas))
    for e in range(tall):
        line = block[e // per : e // per + 1, :]
        if e % per:
            line = pltpu.roll(line, LANES - (e % per) * wide, axis=1)
        weight_grad[e : e + 1, :] = line[:, :wide]

    wait_all(out_send, send_sems.at[0], groups - 1)
    wait_all(ret_send, send_sems.at[3], groups - 1)
    wait_all(tile_send, send_sems.at[4], replicas - 1)
    wait_all(z_send, send_sems.at[5], chips - 1)


def body(
    groups, replicas, features, neighbours, send_rows, send_counts, candidates, perturbation, weight
):
    rows, width = features.shape[1:]
    capacity = send_rows.shape[3]
    queries, cands = candidates.shape[1:]
    samples = perturbation.shape[2]
    slots = groups * capacity
    parts = capacity * width // LANES
    tall, wide = width // groups, width // replicas
    chips = groups // 2
    half = tall * chips
    packed = tall * wide // LANES
    vmem = pl.BlockSpec(memory_space=pltpu.VMEM)
    message = pltpu.VMEM((groups, parts, LANES), BF16)
    d_features, weight_grad = pl.pallas_call(
        functools.partial(kernel, groups, replicas),
        name="layer",
        out_shape=(
            jax.ShapeDtypeStruct((rows, width), BF16),
            jax.ShapeDtypeStruct((tall, wide), F32),
        ),
        in_specs=[vmem] * 7,
        out_specs=(vmem, vmem),
        scratch_shapes=[
            pltpu.VMEM((groups * parts, LANES), F32),
            message,
            message,
            message,
            message,
            pltpu.VMEM((rows, half), BF16),
            pltpu.VMEM((rows, half), BF16),
            pltpu.VMEM((rows, width), BF16),
            pltpu.VMEM((rows, width), BF16),
            pltpu.VMEM((replicas, wide, half), BF16),
            pltpu.VMEM((replicas, wide, half), BF16),
            pltpu.VMEM((chips, packed, LANES), F32),
            pltpu.VMEM((chips, packed, LANES), F32),
            pltpu.VMEM((rows, rows + slots), BF16),
            pltpu.VMEM((rows + slots, rows), BF16),
            pltpu.VMEM((queries * rows, cands), BF16),
            pltpu.VMEM((samples, queries, cands), F32),
            pltpu.VMEM((rows, width), F32),
            pltpu.SemaphoreType.DMA((6,)),
            pltpu.SemaphoreType.DMA((6,)),
        ],
        compiler_params=pltpu.CompilerParams(
            collective_id=0, has_side_effects=True, vmem_limit_bytes=40 * 1024 * 1024
        ),
    )(
        features[0],
        neighbours[0].T,
        send_rows[0, 0].T,
        send_counts[0],
        candidates[0],
        perturbation[0],
        weight,
    )
    return d_features[None], weight_grad


def solution(mesh):
    placed = (
        P("replica", "graph", None),
        P("replica", "graph", None),
        P("replica", "graph", None, None),
        P("replica", "graph", None),
        P("replica", "graph", None),
        P("replica", "graph", None, None),
        P(),
    )
    return jax.shard_map(
        functools.partial(body, mesh.shape["graph"], mesh.shape["replica"]),
        mesh=mesh,
        in_specs=placed,
        out_specs=(P("replica", "graph", None), P("graph", "replica")),
        check_vma=False,
    )
```

```python
import functools
import math

import jax
import jax.numpy as jnp
from jax import lax
from jax.experimental import pallas as pl
from jax.experimental.pallas import tpu as pltpu
from jax.sharding import PartitionSpec as P

TOP = 20
SCORE_SCALE = 16.0
LOSS_SCALE = 16.0
EPSILON = 1e-05
LANES = 128
MESH = pl.DeviceIdType.MESH
F32 = jnp.float32
BF16 = jnp.bfloat16


def iota(shape, axis):
    return lax.broadcasted_iota(jnp.int32, shape, axis)


def one_hot(mask):
    return jnp.where(mask, 1.0, 0.0).astype(BF16)


def dot(a, b, a_axis=1, b_axis=0):
    return lax.dot_general(
        a, b, (((a_axis,), (b_axis,)), ((), ())), preferred_element_type=F32
    )


def wait_all(ref, sem, count):
    part = ref.at[pl.ds(0, count)]
    pltpu.make_async_copy(part, part, sem).wait()


def kernel(
    groups,
    replicas,
    features,
    neighbours,
    send_rows,
    counts,
    candidates,
    perturbation,
    weight,
    d_features,
    weight_grad,
    feature_buf,
    neighbour_buf,
    row_buf,
    count_buf,
    candidate_buf,
    noise_buf,
    weight_buf,
    stage,
    out_send,
    out_recv,
    relay,
    ret_send,
    ret_recv,
    mean_send,
    mean_recv,
    dpre_send,
    dpre_recv,
    tile_send,
    tile_recv,
    z_send,
    z_recv,
    adj,
    adj_t,
    picks,
    noise,
    total,
    send_sems,
    recv_sems,
    load_sems,
    relay_sems,
):
    mg = lax.axis_index("graph")
    mr = lax.axis_index("replica")
    core = lax.rem(mg, 2)
    chip = lax.div(mg, 2)
    chips = groups // 2
    partner = chip * 2 + 1 - core
    rows, width = features.shape
    fanout = neighbours.shape[0]
    capacity = send_rows.shape[0]
    queries, cands = candidates.shape
    samples = perturbation.shape[1]
    blocks = width // LANES
    parts = capacity * blocks
    slots = groups * capacity
    tall, wide = weight_grad.shape
    half = tall * chips

    near = chips // 4

    barrier = pltpu.get_barrier_semaphore()

    def greet(g, r):
        pl.semaphore_signal(barrier, inc=1, device_id=(g, r), device_id_type=MESH)

    def beside(i):
        return lax.rem(2 * chip + i, groups)

    def greet_near(i, carry):
        greet(beside(2 * near + 1 - i), mr)
        greet(beside(groups - 2 * near + i), mr)
        return carry

    def greet_replica(i, carry):
        greet(mg, lax.rem(mr + i, replicas))
        return carry

    lax.fori_loop(0, 2 * near, greet_near, 0)
    greet(partner, mr)
    lax.fori_loop(1, replicas, greet_replica, 0)

    loads = [
        pltpu.make_async_copy(source, target, load_sems.at[n])
        for n, (source, target) in enumerate(
            (
                (features, feature_buf),
                (send_rows, row_buf),
                (neighbours, neighbour_buf),
                (counts, count_buf),
                (candidates, candidate_buf),
                (perturbation, noise_buf),
                (weight, weight_buf),
            )
        )
    ]
    for load in loads:
        load.start()

    def remote(source, target, slot, g, r):
        return pltpu.make_async_remote_copy(
            src_ref=source,
            dst_ref=target,
            send_sem=send_sems.at[slot],
            recv_sem=recv_sems.at[slot],
            device_id=(g, r),
            device_id_type=MESH,
        )

    def line_up(i):
        return jnp.where(i < chips // 2, i, chips + chips // 2 - 1 - i)

    def pack(values, target):
        for k in range(capacity):
            for j in range(blocks):
                stage[pl.ds(k * blocks + j, groups, stride=parts), :] = values[
                    k * groups : (k + 1) * groups, j * LANES : (j + 1) * LANES
                ]
        target[0:groups] = stage[...].reshape(groups, parts, LANES).astype(BF16)

    def unpack(source):
        stage[...] = source[...].astype(F32).reshape(groups * parts, LANES)
        return jnp.concatenate(
            [
                jnp.concatenate(
                    [
                        stage[pl.ds(k * blocks + j, groups, stride=parts), :]
                        for j in range(blocks)
                    ],
                    axis=1,
                )
                for k in range(capacity)
            ],
            axis=0,
        ).astype(BF16)

    loads[0].wait()
    loads[1].wait()
    feature_rows = feature_buf[...]
    row_of = iota((rows, groups), 0)
    sent = [one_hot(row_of == row_buf[k : k + 1, :]) for k in range(capacity)]
    pack(
        jnp.concatenate([dot(s, feature_rows, 0, 0) for s in sent], axis=0), out_send
    )
    out_send[groups : 2 * groups] = out_send[0:groups]
    out_recv[mg] = out_send[mg]

    loads[2].wait()
    loads[3].wait()
    table = rows + slots
    place = iota((table, rows), 0)
    past = place - rows
    slot_id = rows + capacity * lax.rem(past, groups) + lax.div(past, groups)
    name = jnp.where(past < 0, place, slot_id)
    counted = jnp.zeros((table, rows), F32)
    for f in range(fanout):
        counted = counted + jnp.where(neighbour_buf[f : f + 1, :] == name, 1.0, 0.0)
    count_column = jnp.sum(
        jnp.where(iota((groups, groups), 0) == iota((groups, groups), 1), count_buf[...], 0),
        axis=1,
        keepdims=True,
    )
    keep = jnp.concatenate(
        [jnp.ones((rows, 1), F32)]
        + [jnp.where(count_column > k, 1.0, 0.0) for k in range(capacity)],
        axis=0,
    )
    counted = counted * keep
    adj_t[...] = counted.astype(BF16)
    adj[...] = counted.T.astype(BF16)
    loads[4].wait()
    node = iota((rows, cands), 0)

    def pick(q, carry):
        picks[pl.ds(pl.multiple_of(q * rows, rows), rows), :] = one_hot(
            candidate_buf[pl.ds(q, 1), :] == node
        )
        return carry

    lax.fori_loop(0, queries, pick, 0)
    loads[5].wait()
    for m in range(samples):
        noise[m] = noise_buf[:, m, :]
    total[...] = feature_rows.astype(F32) + dot(adj[:, :rows], feature_rows)
    column = iota((width, half), 0)
    order = iota((width, half), 1)
    wing = chips // 2
    lanes = tall * wing
    wanted = (lax.div(order, lanes) * wing + lax.rem(order, wing)) * 2 * tall + lax.rem(
        lax.div(order, wing), tall
    )
    mine = one_hot(column == wanted + core * tall)
    theirs = one_hot(column == wanted + (1 - core) * tall)

    loads[6].wait()

    pl.semaphore_wait(barrier, 4 * near + replicas)
    after, before = beside(2 * near + core), beside(groups - 2 * near + core)

    def relayed(side, k, first, count):
        return relay.at[side, pl.ds(2 * (k - near - 1) + first, count)]

    def launch(side, k, first=0, count=2):
        row = 2 * k if side == 0 else groups - 2 * k
        pltpu.make_async_remote_copy(
            src_ref=out_send.at[pl.ds(2 * chip + row + first, count)],
            dst_ref=relayed(side, k, first, count),
            send_sem=send_sems.at[7],
            recv_sem=relay_sems.at[side, k - near - 1],
            device_id=(after if side == 0 else before, mr),
            device_id_type=MESH,
        ).start()

    def forward(side, k, first=0, count=2):
        part = relayed(side, k, first, count)
        pltpu.make_async_copy(part, part, relay_sems.at[side, k - near - 1]).wait()
        place = 2 * (k - near) if side == 0 else groups - 2 * (k - near)
        source = before if side == 0 else after
        for c in range(first, first + count):
            remote(
                relay.at[side, 2 * (k - near - 1) + c],
                out_recv.at[source],
                0,
                beside(place + c),
                mr,
            ).start()

    def farther(step):
        step(0, 2 * near, 0, 1)
        step(1, 2 * near, 1, 1)

        def both(i, carry):
            step(0, 2 * near - 1 - i)
            step(1, 2 * near - 1 - i)
            return carry

        lax.fori_loop(0, near - 1, both, 0)

    def direct(i):
        remote(out_send.at[2 * chip + i], out_recv.at[mg], 0, beside(i), mr).start()

    def send_near(i, carry):
        direct(2 * near + 1 - i)
        direct(groups - 2 * near + i)
        return carry

    farther(launch)
    lax.fori_loop(0, near, send_near, 0)
    direct(1 - core)
    farther(forward)
    lax.fori_loop(near, 2 * near, send_near, 0)

    wait_all(out_recv, recv_sems.at[0], groups - 1)
    halo = unpack(out_recv)
    scale = 1.0 / (fanout + 1)
    mean_rows = ((total[...] + dot(adj[:, rows:], halo)) * scale).astype(BF16)
    pre = dot(mean_rows, weight_buf[...])
    inverse = lax.rsqrt(jnp.mean(pre * pre, axis=-1, keepdims=True) + EPSILON)
    embedded = (pre * inverse).astype(BF16)

    mean_send[...] = dot(mean_rows, theirs).astype(BF16)
    mean_copy = remote(mean_send, mean_recv, 1, partner, mr)
    mean_copy.start()
    mean_mine = dot(mean_rows, mine).astype(BF16)

    factor = SCORE_SCALE / width
    similar = factor * dot(embedded[:queries], embedded, 1, 1)
    scores = jnp.concatenate(
        [
            jnp.take_along_axis(
                similar,
                candidate_buf[:, c * rows : (c + 1) * rows],
                axis=1,
                mode="promise_in_bounds",
            )
            for c in range(cands // rows)
        ],
        axis=1,
    )
    soft = jnp.zeros((queries, cands), F32)
    for m in range(samples):
        shifted = scores + noise[m]
        exponent = jnp.exp(shifted - jnp.max(shifted, axis=-1, keepdims=True))
        soft = soft + exponent * (1.0 / jnp.sum(exponent, axis=-1, keepdims=True))
    engaged = jnp.where(iota((queries, cands), 1) < TOP, LOSS_SCALE, 0.0)
    d_scores = (LOSS_SCALE * TOP / samples) * soft - engaged
    high = d_scores.astype(BF16)
    low = (d_scores - high.astype(F32)).astype(BF16)
    both = jnp.concatenate(
        [high, low, jnp.zeros((LANES - 2 * queries, cands), BF16)], axis=0
    )
    lane = iota((rows, LANES), 1)
    spread = jnp.zeros((rows, LANES), F32)
    group = 8
    for g in range(queries // group):
        some = dot(picks[g * group * rows : (g + 1) * group * rows, :], both, 1, 1)
        for i in range(group):
            q = g * group + i
            spread = spread + jnp.where(
                lax.rem(lane, queries) == q, some[i * rows : (i + 1) * rows, :], 0.0
            )
    spread = spread + pltpu.roll(spread, LANES - queries, axis=1)
    similar_t = jnp.where(lane < queries, spread, 0.0).astype(BF16).astype(F32)
    mixed = jnp.concatenate([similar_t, similar_t.T], axis=1).astype(BF16)
    d_embedded = factor * dot(mixed, jnp.concatenate([embedded, embedded], axis=0))
    slope = jnp.mean(d_embedded * pre, axis=-1, keepdims=True)
    d_pre = (inverse * d_embedded - inverse * inverse * inverse * pre * slope).astype(BF16)
    dpre_send[...] = d_pre
    dpre_copy = remote(dpre_send, dpre_recv, 2, partner, mr)
    dpre_copy.start()

    share = (dot(d_pre, weight_buf[...], 1, 1) * scale).astype(BF16)
    pack(dot(adj_t[rows:, :], share), ret_send)
    ret_recv[mg] = ret_send[mg]

    def send_back(i, carry):
        peer = 2 * line_up(lax.div(i, 2)) + lax.rem(i, 2)

        @pl.when(peer != mg)
        def _():
            remote(ret_send.at[peer], ret_recv.at[mg], 3, peer, mr).start()

        return carry

    soon = 3 * near // 2
    lax.fori_loop(0, soon, send_back, 0)

    product = dot(d_pre, mean_mine, 0, 0)
    mean_copy.wait()
    dpre_copy.wait()

    def send_tiles(side):
        part = slice(side * lanes, (side + 1) * lanes)
        both = product[:, part] + dot(dpre_recv[...], mean_recv[:, part], 0, 0)
        tile_send[side] = both.astype(BF16).reshape(replicas, wide, lanes)
        tile_recv[side, mr] = tile_send[side, mr]

        def send_tile(i, carry):
            peer = lax.rem(mr + i, replicas)
            remote(
                tile_send.at[side, peer], tile_recv.at[side, mr], 4 + side, mg, peer
            ).start()
            return carry

        lax.fori_loop(1, replicas, send_tile, 0)

    send_tiles(0)
    send_tiles(1)

    def send_z(i, carry):
        peer = line_up(i)

        @pl.when(peer != chip)
        def _():
            remote(z_send.at[peer], z_recv.at[chip], 6, 2 * peer + core, mr).start()

        return carry

    total[...] = share.astype(F32) + dot(adj_t[:rows, :], share)
    per = LANES // wide

    def plane_sum(side):
        wait_all(tile_recv.at[side], recv_sems.at[4 + side], replicas - 1)
        plane = tile_recv[side, 0].astype(F32)
        for p in range(1, replicas):
            plane = plane + tile_recv[side, p].astype(F32)
        if wide < LANES:
            plane = jnp.concatenate([plane, jnp.zeros((LANES - wide, lanes), F32)], axis=0)
        plane_t = plane.T
        for h in range(tall // per):
            packed = plane_t[h * per * wing : (h * per + 1) * wing, :]
            for i in range(1, per):
                e = h * per + i
                packed = packed + pltpu.roll(
                    plane_t[e * wing : (e + 1) * wing, :], i * wide, axis=1
                )
            for c in range(wing):
                z_send[side * wing + c, h : h + 1, :] = packed[c : c + 1, :]

    plane_sum(0)
    lax.fori_loop(0, wing, send_z, 0)
    lax.fori_loop(soon, 2 * wing, send_back, 0)
    plane_sum(1)
    lax.fori_loop(wing, chips, send_z, 0)
    lax.fori_loop(2 * wing, groups, send_back, 0)
    z_recv[chip] = z_send[chip]

    wait_all(ret_recv, recv_sems.at[3], groups - 1)
    returned = unpack(ret_recv)
    d_rows = total[...]
    for k in range(capacity):
        d_rows = d_rows + dot(sent[k], returned[k * groups : (k + 1) * groups, :])
    d_features[...] = d_rows.astype(BF16)

    wait_all(z_recv, recv_sems.at[6], chips - 1)
    block = jnp.sum(z_recv[...], axis=0) * (1.0 / math.sqrt(groups * replicas))
    for e in range(tall):
        line = block[e // per : e // per + 1, :]
        if e % per:
            line = pltpu.roll(line, LANES - (e % per) * wide, axis=1)
        weight_grad[e : e + 1, :] = line[:, :wide]

    wait_all(out_send, send_sems.at[7], 4 * near - 2)
    wait_all(out_send, send_sems.at[0], groups - 1)
    wait_all(ret_send, send_sems.at[3], groups - 1)
    wait_all(tile_send.at[0], send_sems.at[4], replicas - 1)
    wait_all(tile_send.at[1], send_sems.at[5], replicas - 1)
    wait_all(z_send, send_sems.at[6], chips - 1)


def hand_over(rows, block, rows_out, block_out):
    rows_out[...] = rows[...]
    block_out[...] = block[...]


def body(
    groups, replicas, features, neighbours, send_rows, send_counts, candidates, perturbation, weight
):
    rows, width = features.shape[1:]
    capacity = send_rows.shape[3]
    queries, cands = candidates.shape[1:]
    samples = perturbation.shape[2]
    slots = groups * capacity
    parts = capacity * width // LANES
    tall, wide = width // groups, width // replicas
    chips = groups // 2
    half = tall * chips
    packed = tall * wide // LANES
    args = (
        features[0],
        neighbours[0].T,
        send_rows[0, 0].T,
        send_counts[0],
        candidates[0],
        perturbation[0],
        weight,
    )
    vmem = pl.BlockSpec(memory_space=pltpu.VMEM)
    message = pltpu.VMEM((groups, parts, LANES), BF16)
    d_features, weight_grad = pl.pallas_call(
        functools.partial(kernel, groups, replicas),
        name="layer",
        out_shape=(
            jax.ShapeDtypeStruct((rows, width), BF16),
            jax.ShapeDtypeStruct((tall, wide), F32),
        ),
        in_specs=[pl.BlockSpec(memory_space=pl.ANY)] * 7,
        out_specs=(vmem, vmem),
        scratch_shapes=[pltpu.VMEM(x.shape, x.dtype) for x in args]
        + [
            pltpu.VMEM((groups * parts, LANES), F32),
            pltpu.VMEM((2 * groups, parts, LANES), BF16),
            message,
            pltpu.VMEM((2, chips // 2, parts, LANES), BF16),
            message,
            message,
            pltpu.VMEM((rows, half), BF16),
            pltpu.VMEM((rows, half), BF16),
            pltpu.VMEM((rows, width), BF16),
            pltpu.VMEM((rows, width), BF16),
            pltpu.VMEM((2, replicas, wide, half // 2), BF16),
            pltpu.VMEM((2, replicas, wide, half // 2), BF16),
            pltpu.VMEM((chips, packed, LANES), F32),
            pltpu.VMEM((chips, packed, LANES), F32),
            pltpu.VMEM((rows, rows + slots), BF16),
            pltpu.VMEM((rows + slots, rows), BF16),
            pltpu.VMEM((queries * rows, cands), BF16),
            pltpu.VMEM((samples, queries, cands), F32),
            pltpu.VMEM((rows, width), F32),
            pltpu.SemaphoreType.DMA((8,)),
            pltpu.SemaphoreType.DMA((8,)),
            pltpu.SemaphoreType.DMA((7,)),
            pltpu.SemaphoreType.DMA((2, chips // 4)),
        ],
        compiler_params=pltpu.CompilerParams(
            collective_id=0, has_side_effects=True, vmem_limit_bytes=56 * 1024 * 1024
        ),
    )(*args)
    d_features, weight_grad = pl.pallas_call(
        hand_over,
        name="hand_over",
        out_shape=(
            jax.ShapeDtypeStruct((rows, width), BF16),
            jax.ShapeDtypeStruct((tall, wide), F32),
        ),
        in_specs=[vmem] * 2,
        out_specs=(vmem, vmem),
    )(d_features, weight_grad)
    return d_features[None], weight_grad


def solution(mesh):
    placed = (
        P("replica", "graph", None),
        P("replica", "graph", None),
        P("replica", "graph", None, None),
        P("replica", "graph", None),
        P("replica", "graph", None),
        P("replica", "graph", None, None),
        P(),
    )
    return jax.shard_map(
        functools.partial(body, mesh.shape["graph"], mesh.shape["replica"]),
        mesh=mesh,
        in_specs=placed,
        out_specs=(P("replica", "graph", None), P("graph", "replica")),
        check_vma=False,
    )
```

```python
import functools
import math

import jax
import jax.numpy as jnp
from jax import lax
from jax.experimental import pallas as pl
from jax.experimental.pallas import tpu as pltpu
from jax.sharding import PartitionSpec as P

TOP = 20
SCORE_SCALE = 16.0
LOSS_SCALE = 16.0
EPSILON = 1e-05
LANES = 128
MESH = pl.DeviceIdType.MESH
F32 = jnp.float32
BF16 = jnp.bfloat16


def iota(shape, axis):
    return lax.broadcasted_iota(jnp.int32, shape, axis)


def one_hot(mask):
    return jnp.where(mask, 1.0, 0.0).astype(BF16)


def dot(a, b, a_axis=1, b_axis=0):
    return lax.dot_general(
        a, b, (((a_axis,), (b_axis,)), ((), ())), preferred_element_type=F32
    )


def wait_all(ref, sem, count):
    part = ref.at[pl.ds(0, count)]
    pltpu.make_async_copy(part, part, sem).wait()


def kernel(
    groups,
    replicas,
    features,
    neighbours,
    send_rows,
    counts,
    candidates,
    perturbation,
    weight,
    d_features,
    weight_grad,
    feature_buf,
    neighbour_buf,
    row_buf,
    count_buf,
    candidate_buf,
    noise_buf,
    weight_buf,
    stage,
    out_send,
    out_recv,
    relay,
    ret_send,
    ret_recv,
    mean_send,
    mean_recv,
    dpre_send,
    dpre_recv,
    tile_send,
    tile_recv,
    z_send,
    z_recv,
    adj,
    adj_t,
    picks,
    noise,
    total,
    send_sems,
    recv_sems,
    load_sems,
    relay_sems,
):
    mg = lax.axis_index("graph")
    mr = lax.axis_index("replica")
    core = lax.rem(mg, 2)
    chip = lax.div(mg, 2)
    chips = groups // 2
    partner = chip * 2 + 1 - core
    rows, width = features.shape
    fanout = neighbours.shape[0]
    capacity = send_rows.shape[0]
    queries, cands = candidates.shape
    samples = perturbation.shape[1]
    blocks = width // LANES
    parts = capacity * blocks
    slots = groups * capacity
    tall, wide = weight_grad.shape
    half = tall * chips

    near = chips // 4

    barrier = pltpu.get_barrier_semaphore()

    def greet(g, r):
        pl.semaphore_signal(barrier, inc=1, device_id=(g, r), device_id_type=MESH)

    def beside(i):
        return lax.rem(2 * chip + i, groups)

    def greet_near(i, carry):
        greet(beside(2 * near + 1 - i), mr)
        greet(beside(groups - 2 * near + i), mr)
        return carry

    def greet_replica(i, carry):
        greet(mg, lax.rem(mr + i, replicas))
        return carry

    lax.fori_loop(0, 2 * near, greet_near, 0)
    greet(partner, mr)
    lax.fori_loop(1, replicas, greet_replica, 0)

    loads = [
        pltpu.make_async_copy(source, target, load_sems.at[n])
        for n, (source, target) in enumerate(
            (
                (features, feature_buf),
                (send_rows, row_buf),
                (neighbours, neighbour_buf),
                (counts, count_buf),
                (candidates, candidate_buf),
                (perturbation, noise_buf),
                (weight, weight_buf),
            )
        )
    ]
    for load in loads:
        load.start()

    def remote(source, target, slot, g, r):
        return pltpu.make_async_remote_copy(
            src_ref=source,
            dst_ref=target,
            send_sem=send_sems.at[slot],
            recv_sem=recv_sems.at[slot],
            device_id=(g, r),
            device_id_type=MESH,
        )

    def line_up(i):
        return jnp.where(i < chips // 2, i, chips + chips // 2 - 1 - i)

    def pack(values, target):
        for k in range(capacity):
            for j in range(blocks):
                stage[pl.ds(k * blocks + j, groups, stride=parts), :] = values[
                    k * groups : (k + 1) * groups, j * LANES : (j + 1) * LANES
                ]
        target[0:groups] = stage[...].reshape(groups, parts, LANES).astype(BF16)

    def unpack(source):
        stage[...] = source[...].astype(F32).reshape(groups * parts, LANES)
        return jnp.concatenate(
            [
                jnp.concatenate(
                    [
                        stage[pl.ds(k * blocks + j, groups, stride=parts), :]
                        for j in range(blocks)
                    ],
                    axis=1,
                )
                for k in range(capacity)
            ],
            axis=0,
        ).astype(BF16)

    loads[0].wait()
    loads[1].wait()
    feature_rows = feature_buf[...]
    row_of = iota((rows, groups), 0)
    sent = [one_hot(row_of == row_buf[k : k + 1, :]) for k in range(capacity)]
    pack(
        jnp.concatenate([dot(s, feature_rows, 0, 0) for s in sent], axis=0), out_send
    )
    out_send[groups : 2 * groups] = out_send[0:groups]
    out_recv[mg] = out_send[mg]

    loads[2].wait()
    loads[3].wait()
    table = rows + slots
    place = iota((table, rows), 0)
    past = place - rows
    slot_id = rows + capacity * lax.rem(past, groups) + lax.div(past, groups)
    name = jnp.where(past < 0, place, slot_id)
    counted = jnp.zeros((table, rows), F32)
    for f in range(fanout):
        counted = counted + jnp.where(neighbour_buf[f : f + 1, :] == name, 1.0, 0.0)
    count_column = jnp.sum(
        jnp.where(iota((groups, groups), 0) == iota((groups, groups), 1), count_buf[...], 0),
        axis=1,
        keepdims=True,
    )
    keep = jnp.concatenate(
        [jnp.ones((rows, 1), F32)]
        + [jnp.where(count_column > k, 1.0, 0.0) for k in range(capacity)],
        axis=0,
    )
    counted = counted * keep
    adj_t[...] = counted.astype(BF16)
    adj[...] = counted.T.astype(BF16)
    loads[4].wait()
    node = iota((rows, cands), 0)

    def pick(q, carry):
        picks[pl.ds(pl.multiple_of(q * rows, rows), rows), :] = one_hot(
            candidate_buf[pl.ds(q, 1), :] == node
        )
        return carry

    lax.fori_loop(0, queries, pick, 0)
    loads[5].wait()
    for m in range(samples):
        noise[m] = noise_buf[:, m, :]
    total[...] = feature_rows.astype(F32) + dot(adj[:, :rows], feature_rows)
    column = iota((width, half), 0)
    order = iota((width, half), 1)
    wing = chips // 2
    lanes = tall * wing
    wanted = (lax.div(order, lanes) * wing + lax.rem(order, wing)) * 2 * tall + lax.rem(
        lax.div(order, wing), tall
    )
    mine = one_hot(column == wanted + core * tall)
    theirs = one_hot(column == wanted + (1 - core) * tall)

    loads[6].wait()

    pl.semaphore_wait(barrier, 4 * near + replicas)
    after, before = beside(2 * near + core), beside(groups - 2 * near + core)

    def relayed(side, k, first, count):
        return relay.at[side, pl.ds(2 * (k - near - 1) + first, count)]

    def launch(side, k, first=0, count=2):
        row = 2 * k if side == 0 else groups - 2 * k
        pltpu.make_async_remote_copy(
            src_ref=out_send.at[pl.ds(2 * chip + row + first, count)],
            dst_ref=relayed(side, k, first, count),
            send_sem=send_sems.at[7],
            recv_sem=relay_sems.at[side, k - near - 1],
            device_id=(after if side == 0 else before, mr),
            device_id_type=MESH,
        ).start()

    def forward(side, k, first=0, count=2):
        part = relayed(side, k, first, count)
        pltpu.make_async_copy(part, part, relay_sems.at[side, k - near - 1]).wait()
        place = 2 * (k - near) if side == 0 else groups - 2 * (k - near)
        source = before if side == 0 else after
        for c in range(first, first + count):
            remote(
                relay.at[side, 2 * (k - near - 1) + c],
                out_recv.at[source],
                0,
                beside(place + c),
                mr,
            ).start()

    def farther(step):
        step(0, 2 * near, 0, 1)
        step(1, 2 * near, 1, 1)

        def both(i, carry):
            step(0, 2 * near - 1 - i)
            step(1, 2 * near - 1 - i)
            return carry

        lax.fori_loop(0, near - 1, both, 0)

    def direct(i):
        remote(out_send.at[2 * chip + i], out_recv.at[mg], 0, beside(i), mr).start()

    def send_near(i, carry):
        direct(2 * near + 1 - i)
        direct(groups - 2 * near + i)
        return carry

    farther(launch)
    lax.fori_loop(0, near, send_near, 0)
    direct(1 - core)
    farther(forward)
    lax.fori_loop(near, 2 * near, send_near, 0)

    wait_all(out_recv, recv_sems.at[0], groups - 1)
    halo = unpack(out_recv)
    scale = 1.0 / (fanout + 1)
    mean_rows = ((total[...] + dot(adj[:, rows:], halo)) * scale).astype(BF16)
    pre = dot(mean_rows, weight_buf[...])
    inverse = lax.rsqrt(jnp.mean(pre * pre, axis=-1, keepdims=True) + EPSILON)
    embedded = (pre * inverse).astype(BF16)

    mean_send[...] = dot(mean_rows, theirs).astype(BF16)
    mean_copy = remote(mean_send, mean_recv, 1, partner, mr)
    mean_copy.start()
    mean_mine = dot(mean_rows, mine).astype(BF16)

    factor = SCORE_SCALE / width
    similar = factor * dot(embedded[:queries], embedded, 1, 1)
    scores = jnp.concatenate(
        [
            jnp.take_along_axis(
                similar,
                candidate_buf[:, c * rows : (c + 1) * rows],
                axis=1,
                mode="promise_in_bounds",
            )
            for c in range(cands // rows)
        ],
        axis=1,
    )
    soft = jnp.zeros((queries, cands), F32)
    for m in range(samples):
        shifted = scores + noise[m]
        exponent = jnp.exp(shifted - jnp.max(shifted, axis=-1, keepdims=True))
        soft = soft + exponent * (1.0 / jnp.sum(exponent, axis=-1, keepdims=True))
    engaged = jnp.where(iota((queries, cands), 1) < TOP, LOSS_SCALE, 0.0)
    d_scores = (LOSS_SCALE * TOP / samples) * soft - engaged
    high = d_scores.astype(BF16)
    low = (d_scores - high.astype(F32)).astype(BF16)
    both = jnp.concatenate(
        [high, low, jnp.zeros((LANES - 2 * queries, cands), BF16)], axis=0
    )
    lane = iota((rows, LANES), 1)
    spread = jnp.zeros((rows, LANES), F32)
    group = 8
    for g in range(queries // group):
        some = dot(picks[g * group * rows : (g + 1) * group * rows, :], both, 1, 1)
        for i in range(group):
            q = g * group + i
            spread = spread + jnp.where(
                lax.rem(lane, queries) == q, some[i * rows : (i + 1) * rows, :], 0.0
            )
    spread = spread + pltpu.roll(spread, LANES - queries, axis=1)
    similar_t = jnp.where(lane < queries, spread, 0.0).astype(BF16).astype(F32)
    mixed = jnp.concatenate([similar_t, similar_t.T], axis=1).astype(BF16)
    d_embedded = factor * dot(mixed, jnp.concatenate([embedded, embedded], axis=0))
    slope = jnp.mean(d_embedded * pre, axis=-1, keepdims=True)
    d_pre = (inverse * d_embedded - inverse * inverse * inverse * pre * slope).astype(BF16)
    dpre_send[...] = d_pre
    dpre_copy = remote(dpre_send, dpre_recv, 2, partner, mr)
    dpre_copy.start()

    def send_back(i, carry):
        peer = 2 * line_up(lax.div(i, 2)) + lax.rem(i, 2)

        @pl.when(peer != mg)
        def _():
            remote(ret_send.at[peer], ret_recv.at[mg], 3, peer, mr).start()

        return carry


    product = dot(d_pre, mean_mine, 0, 0)
    mean_copy.wait()
    dpre_copy.wait()

    across = math.isqrt(replicas)
    steps = sorted(
        ((dx, dy) for dx in range(across) for dy in range(across) if dx or dy),
        key=lambda step: (
            -sum(min(d, across - d) for d in step),
            min(step[0], across - step[0]) - min(step[1], across - step[1]),
        ),
    )

    def send_tiles(side):
        part = slice(side * lanes, (side + 1) * lanes)
        both = product[:, part] + dot(dpre_recv[...], mean_recv[:, part], 0, 0)
        tile_send[side] = both.astype(BF16).reshape(replicas, wide, lanes)
        tile_recv[side, mr] = tile_send[side, mr]

        for dx, dy in steps:
            peer = lax.rem(mr // across + dx, across) * across + lax.rem(mr + dy, across)
            remote(
                tile_send.at[side, peer], tile_recv.at[side, mr], 4 + side, mg, peer
            ).start()

    send_tiles(0)
    send_tiles(1)

    share = (dot(d_pre, weight_buf[...], 1, 1) * scale).astype(BF16)
    pack(dot(adj_t[rows:, :], share), ret_send)
    ret_recv[mg] = ret_send[mg]


    def send_z(i, carry):
        peer = line_up(i)

        @pl.when(peer != chip)
        def _():
            remote(z_send.at[peer], z_recv.at[chip], 6, 2 * peer + core, mr).start()

        return carry

    total[...] = share.astype(F32) + dot(adj_t[:rows, :], share)
    per = LANES // wide

    def plane_sum(side):
        wait_all(tile_recv.at[side], recv_sems.at[4 + side], replicas - 1)
        plane = tile_recv[side, 0].astype(F32)
        for p in range(1, replicas):
            plane = plane + tile_recv[side, p].astype(F32)
        if wide < LANES:
            plane = jnp.concatenate([plane, jnp.zeros((LANES - wide, lanes), F32)], axis=0)
        plane_t = plane.T
        for h in range(tall // per):
            packed = plane_t[h * per * wing : (h * per + 1) * wing, :]
            for i in range(1, per):
                e = h * per + i
                packed = packed + pltpu.roll(
                    plane_t[e * wing : (e + 1) * wing, :], i * wide, axis=1
                )
            for c in range(wing):
                z_send[side * wing + c, h : h + 1, :] = packed[c : c + 1, :]

    soon = 16
    lax.fori_loop(0, soon, send_back, 0)
    plane_sum(0)
    lax.fori_loop(0, wing, send_z, 0)
    lax.fori_loop(soon, 2 * wing, send_back, 0)
    plane_sum(1)
    lax.fori_loop(wing, chips, send_z, 0)
    lax.fori_loop(2 * wing, groups, send_back, 0)
    z_recv[chip] = z_send[chip]

    wait_all(ret_recv, recv_sems.at[3], groups - 1)
    returned = unpack(ret_recv)
    d_rows = total[...]
    for k in range(capacity):
        d_rows = d_rows + dot(sent[k], returned[k * groups : (k + 1) * groups, :])
    d_features[...] = d_rows.astype(BF16)

    wait_all(z_recv, recv_sems.at[6], chips - 1)
    block = jnp.sum(z_recv[...], axis=0) * (1.0 / math.sqrt(groups * replicas))
    for e in range(tall):
        line = block[e // per : e // per + 1, :]
        if e % per:
            line = pltpu.roll(line, LANES - (e % per) * wide, axis=1)
        weight_grad[e : e + 1, :] = line[:, :wide]

    wait_all(out_send, send_sems.at[7], 4 * near - 2)
    wait_all(out_send, send_sems.at[0], groups - 1)
    wait_all(ret_send, send_sems.at[3], groups - 1)
    wait_all(tile_send.at[0], send_sems.at[4], replicas - 1)
    wait_all(tile_send.at[1], send_sems.at[5], replicas - 1)
    wait_all(z_send, send_sems.at[6], chips - 1)


def hand_over(rows, block, rows_out, block_out):
    rows_out[...] = rows[...]
    block_out[...] = block[...]


def body(
    groups, replicas, features, neighbours, send_rows, send_counts, candidates, perturbation, weight
):
    rows, width = features.shape[1:]
    capacity = send_rows.shape[3]
    queries, cands = candidates.shape[1:]
    samples = perturbation.shape[2]
    slots = groups * capacity
    parts = capacity * width // LANES
    tall, wide = width // groups, width // replicas
    chips = groups // 2
    half = tall * chips
    packed = tall * wide // LANES
    args = (
        features[0],
        neighbours[0].T,
        send_rows[0, 0].T,
        send_counts[0],
        candidates[0],
        perturbation[0],
        weight,
    )
    vmem = pl.BlockSpec(memory_space=pltpu.VMEM)
    message = pltpu.VMEM((groups, parts, LANES), BF16)
    d_features, weight_grad = pl.pallas_call(
        functools.partial(kernel, groups, replicas),
        name="layer",
        out_shape=(
            jax.ShapeDtypeStruct((rows, width), BF16),
            jax.ShapeDtypeStruct((tall, wide), F32),
        ),
        in_specs=[pl.BlockSpec(memory_space=pl.ANY)] * 7,
        out_specs=(vmem, vmem),
        scratch_shapes=[pltpu.VMEM(x.shape, x.dtype) for x in args]
        + [
            pltpu.VMEM((groups * parts, LANES), F32),
            pltpu.VMEM((2 * groups, parts, LANES), BF16),
            message,
            pltpu.VMEM((2, chips // 2, parts, LANES), BF16),
            message,
            message,
            pltpu.VMEM((rows, half), BF16),
            pltpu.VMEM((rows, half), BF16),
            pltpu.VMEM((rows, width), BF16),
            pltpu.VMEM((rows, width), BF16),
            pltpu.VMEM((2, replicas, wide, half // 2), BF16),
            pltpu.VMEM((2, replicas, wide, half // 2), BF16),
            pltpu.VMEM((chips, packed, LANES), F32),
            pltpu.VMEM((chips, packed, LANES), F32),
            pltpu.VMEM((rows, rows + slots), BF16),
            pltpu.VMEM((rows + slots, rows), BF16),
            pltpu.VMEM((queries * rows, cands), BF16),
            pltpu.VMEM((samples, queries, cands), F32),
            pltpu.VMEM((rows, width), F32),
            pltpu.SemaphoreType.DMA((8,)),
            pltpu.SemaphoreType.DMA((8,)),
            pltpu.SemaphoreType.DMA((7,)),
            pltpu.SemaphoreType.DMA((2, chips // 4)),
        ],
        compiler_params=pltpu.CompilerParams(
            collective_id=0, has_side_effects=True, vmem_limit_bytes=56 * 1024 * 1024
        ),
    )(*args)
    d_features, weight_grad = pl.pallas_call(
        hand_over,
        name="hand_over",
        out_shape=(
            jax.ShapeDtypeStruct((rows, width), BF16),
            jax.ShapeDtypeStruct((tall, wide), F32),
        ),
        in_specs=[vmem] * 2,
        out_specs=(vmem, vmem),
    )(d_features, weight_grad)
    return d_features[None], weight_grad


def solution(mesh):
    placed = (
        P("replica", "graph", None),
        P("replica", "graph", None),
        P("replica", "graph", None, None),
        P("replica", "graph", None),
        P("replica", "graph", None),
        P("replica", "graph", None, None),
        P(),
    )
    return jax.shard_map(
        functools.partial(body, mesh.shape["graph"], mesh.shape["replica"]),
        mesh=mesh,
        in_specs=placed,
        out_specs=(P("replica", "graph", None), P("graph", "replica")),
        check_vma=False,
    )
```

```python
import functools
import math

import jax
import jax.numpy as jnp
from jax import lax
from jax.experimental import pallas as pl
from jax.experimental.pallas import tpu as pltpu
from jax.sharding import PartitionSpec as P

TOP = 20
SCORE_SCALE = 16.0
LOSS_SCALE = 16.0
EPSILON = 1e-05
LANES = 128
MESH = pl.DeviceIdType.MESH
F32 = jnp.float32
BF16 = jnp.bfloat16


def iota(shape, axis):
    return lax.broadcasted_iota(jnp.int32, shape, axis)


def one_hot(mask):
    return jnp.where(mask, 1.0, 0.0).astype(BF16)


def dot(a, b, a_axis=1, b_axis=0):
    return lax.dot_general(
        a, b, (((a_axis,), (b_axis,)), ((), ())), preferred_element_type=F32
    )


def wait_all(ref, sem, count):
    part = ref.at[pl.ds(0, count)]
    pltpu.make_async_copy(part, part, sem).wait()


def kernel(
    groups,
    replicas,
    features,
    neighbours,
    send_rows,
    counts,
    candidates,
    perturbation,
    weight,
    d_features,
    weight_grad,
    feature_buf,
    neighbour_buf,
    row_buf,
    count_buf,
    candidate_buf,
    noise_buf,
    weight_buf,
    stage,
    out_send,
    out_recv,
    relay,
    ret_send,
    ret_recv,
    mean_send,
    mean_recv,
    dpre_send,
    dpre_recv,
    tile_send,
    tile_recv,
    z_send,
    z_recv,
    adj,
    adj_t,
    picks,
    noise,
    total,
    send_sems,
    recv_sems,
    load_sems,
    relay_sems,
    row_out,
):
    mg = lax.axis_index("graph")
    mr = lax.axis_index("replica")
    core = lax.rem(mg, 2)
    chip = lax.div(mg, 2)
    chips = groups // 2
    partner = chip * 2 + 1 - core
    rows, width = features.shape
    fanout = neighbours.shape[0]
    capacity = send_rows.shape[0]
    queries, cands = candidates.shape
    samples = perturbation.shape[1]
    blocks = width // LANES
    parts = capacity * blocks
    slots = groups * capacity
    tall, wide = weight_grad.shape
    half = tall * chips

    near = chips // 4

    barrier = pltpu.get_barrier_semaphore()

    def greet(g, r):
        pl.semaphore_signal(barrier, inc=1, device_id=(g, r), device_id_type=MESH)

    def beside(i):
        return lax.rem(2 * chip + i, groups)

    def greet_near(i, carry):
        greet(beside(2 * near + 1 - i), mr)
        greet(beside(groups - 2 * near + i), mr)
        return carry

    def greet_replica(i, carry):
        greet(mg, lax.rem(mr + i, replicas))
        return carry

    lax.fori_loop(0, 2 * near, greet_near, 0)
    greet(partner, mr)
    lax.fori_loop(1, replicas, greet_replica, 0)

    loads = [
        pltpu.make_async_copy(source, target, load_sems.at[n])
        for n, (source, target) in enumerate(
            (
                (features, feature_buf),
                (send_rows, row_buf),
                (neighbours, neighbour_buf),
                (counts, count_buf),
                (candidates, candidate_buf),
                (perturbation, noise_buf),
                (weight, weight_buf),
            )
        )
    ]
    for load in loads:
        load.start()

    def remote(source, target, slot, g, r):
        return pltpu.make_async_remote_copy(
            src_ref=source,
            dst_ref=target,
            send_sem=send_sems.at[slot],
            recv_sem=recv_sems.at[slot],
            device_id=(g, r),
            device_id_type=MESH,
        )

    def line_up(i):
        return jnp.where(i < chips // 2, i, chips + chips // 2 - 1 - i)

    def pack(values, target):
        for k in range(capacity):
            for j in range(blocks):
                stage[pl.ds(k * blocks + j, groups, stride=parts), :] = values[
                    k * groups : (k + 1) * groups, j * LANES : (j + 1) * LANES
                ]
        target[0:groups] = stage[...].reshape(groups, parts, LANES).astype(BF16)

    def unpack(source):
        stage[...] = source[...].astype(F32).reshape(groups * parts, LANES)
        return jnp.concatenate(
            [
                jnp.concatenate(
                    [
                        stage[pl.ds(k * blocks + j, groups, stride=parts), :]
                        for j in range(blocks)
                    ],
                    axis=1,
                )
                for k in range(capacity)
            ],
            axis=0,
        ).astype(BF16)

    loads[0].wait()
    loads[1].wait()
    feature_rows = feature_buf[...]
    row_of = iota((rows, groups), 0)
    sent = [one_hot(row_of == row_buf[k : k + 1, :]) for k in range(capacity)]
    pack(
        jnp.concatenate([dot(s, feature_rows, 0, 0) for s in sent], axis=0), out_send
    )
    out_send[groups : 2 * groups] = out_send[0:groups]
    out_recv[mg] = out_send[mg]

    loads[2].wait()
    loads[3].wait()
    table = rows + slots
    place = iota((table, rows), 0)
    past = place - rows
    slot_id = rows + capacity * lax.rem(past, groups) + lax.div(past, groups)
    name = jnp.where(past < 0, place, slot_id)
    counted = jnp.zeros((table, rows), F32)
    for f in range(fanout):
        counted = counted + jnp.where(neighbour_buf[f : f + 1, :] == name, 1.0, 0.0)
    count_column = jnp.sum(
        jnp.where(iota((groups, groups), 0) == iota((groups, groups), 1), count_buf[...], 0),
        axis=1,
        keepdims=True,
    )
    keep = jnp.concatenate(
        [jnp.ones((rows, 1), F32)]
        + [jnp.where(count_column > k, 1.0, 0.0) for k in range(capacity)],
        axis=0,
    )
    counted = counted * keep
    adj_t[...] = counted.astype(BF16)
    adj[...] = counted.T.astype(BF16)
    loads[4].wait()
    node = iota((rows, cands), 0)

    def pick(q, carry):
        picks[pl.ds(pl.multiple_of(q * rows, rows), rows), :] = one_hot(
            candidate_buf[pl.ds(q, 1), :] == node
        )
        return carry

    lax.fori_loop(0, queries, pick, 0)
    loads[5].wait()
    for m in range(samples):
        noise[m] = noise_buf[:, m, :]
    total[...] = feature_rows.astype(F32) + dot(adj[:, :rows], feature_rows)
    column = iota((width, half), 0)
    order = iota((width, half), 1)
    wing = chips // 2
    lanes = tall * wing
    wanted = (lax.div(order, lanes) * wing + lax.rem(order, wing)) * 2 * tall + lax.rem(
        lax.div(order, wing), tall
    )
    mine = one_hot(column == wanted + core * tall)
    theirs = one_hot(column == wanted + (1 - core) * tall)

    loads[6].wait()

    pl.semaphore_wait(barrier, 4 * near + replicas)
    after, before = beside(2 * near + core), beside(groups - 2 * near + core)

    def relayed(side, k, first, count):
        return relay.at[side, pl.ds(2 * (k - near - 1) + first, count)]

    def launch(side, k, first=0, count=2):
        row = 2 * k if side == 0 else groups - 2 * k
        pltpu.make_async_remote_copy(
            src_ref=out_send.at[pl.ds(2 * chip + row + first, count)],
            dst_ref=relayed(side, k, first, count),
            send_sem=send_sems.at[7],
            recv_sem=relay_sems.at[side, k - near - 1],
            device_id=(after if side == 0 else before, mr),
            device_id_type=MESH,
        ).start()

    def forward(side, k, first=0, count=2):
        part = relayed(side, k, first, count)
        pltpu.make_async_copy(part, part, relay_sems.at[side, k - near - 1]).wait()
        place = 2 * (k - near) if side == 0 else groups - 2 * (k - near)
        source = before if side == 0 else after
        for c in range(first, first + count):
            remote(
                relay.at[side, 2 * (k - near - 1) + c],
                out_recv.at[source],
                0,
                beside(place + c),
                mr,
            ).start()

    def farther(step):
        step(0, 2 * near, 0, 1)
        step(1, 2 * near, 1, 1)

        def both(i, carry):
            step(0, 2 * near - 1 - i)
            step(1, 2 * near - 1 - i)
            return carry

        lax.fori_loop(0, near - 1, both, 0)

    def direct(i):
        remote(out_send.at[2 * chip + i], out_recv.at[mg], 0, beside(i), mr).start()

    def send_near(i, carry):
        direct(2 * near + 1 - i)
        direct(groups - 2 * near + i)
        return carry

    farther(launch)
    lax.fori_loop(0, near, send_near, 0)
    direct(1 - core)
    farther(forward)
    lax.fori_loop(near, 2 * near, send_near, 0)

    wait_all(out_recv, recv_sems.at[0], groups - 1)
    halo = unpack(out_recv)
    scale = 1.0 / (fanout + 1)
    mean_rows = ((total[...] + dot(adj[:, rows:], halo)) * scale).astype(BF16)
    pre = dot(mean_rows, weight_buf[...])
    inverse = lax.rsqrt(jnp.mean(pre * pre, axis=-1, keepdims=True) + EPSILON)
    embedded = (pre * inverse).astype(BF16)

    mean_send[...] = dot(mean_rows, theirs).astype(BF16)
    mean_copy = remote(mean_send, mean_recv, 1, partner, mr)
    mean_copy.start()
    mean_mine = dot(mean_rows, mine).astype(BF16)

    factor = SCORE_SCALE / width
    similar = factor * dot(embedded[:queries], embedded, 1, 1)
    scores = jnp.concatenate(
        [
            jnp.take_along_axis(
                similar,
                candidate_buf[:, c * rows : (c + 1) * rows],
                axis=1,
                mode="promise_in_bounds",
            )
            for c in range(cands // rows)
        ],
        axis=1,
    )
    soft = jnp.zeros((queries, cands), F32)
    for m in range(samples):
        shifted = scores + noise[m]
        exponent = jnp.exp(shifted - jnp.max(shifted, axis=-1, keepdims=True))
        soft = soft + exponent * (1.0 / jnp.sum(exponent, axis=-1, keepdims=True))
    engaged = jnp.where(iota((queries, cands), 1) < TOP, LOSS_SCALE, 0.0)
    d_scores = (LOSS_SCALE * TOP / samples) * soft - engaged
    high = d_scores.astype(BF16)
    low = (d_scores - high.astype(F32)).astype(BF16)
    both = jnp.concatenate(
        [high, low, jnp.zeros((LANES - 2 * queries, cands), BF16)], axis=0
    )
    lane = iota((rows, LANES), 1)
    spread = jnp.zeros((rows, LANES), F32)
    group = 8
    for g in range(queries // group):
        some = dot(picks[g * group * rows : (g + 1) * group * rows, :], both, 1, 1)
        for i in range(group):
            q = g * group + i
            spread = spread + jnp.where(
                lax.rem(lane, queries) == q, some[i * rows : (i + 1) * rows, :], 0.0
            )
    spread = spread + pltpu.roll(spread, LANES - queries, axis=1)
    similar_t = jnp.where(lane < queries, spread, 0.0).astype(BF16).astype(F32)
    mixed = jnp.concatenate([similar_t, similar_t.T], axis=1).astype(BF16)
    d_embedded = factor * dot(mixed, jnp.concatenate([embedded, embedded], axis=0))
    slope = jnp.mean(d_embedded * pre, axis=-1, keepdims=True)
    d_pre = (inverse * d_embedded - inverse * inverse * inverse * pre * slope).astype(BF16)
    dpre_send[...] = d_pre
    dpre_copy = remote(dpre_send, dpre_recv, 2, partner, mr)
    dpre_copy.start()

    def send_back(i, carry):
        peer = 2 * line_up(lax.div(i, 2)) + lax.rem(i, 2)

        @pl.when(peer != mg)
        def _():
            remote(ret_send.at[peer], ret_recv.at[mg], 3, peer, mr).start()

        return carry


    share = (dot(d_pre, weight_buf[...], 1, 1) * scale).astype(BF16)
    pack(dot(adj_t[rows:, :], share), ret_send)
    ret_recv[mg] = ret_send[mg]


    def send_z(i, carry):
        peer = line_up(i)

        @pl.when(peer != chip)
        def _():
            remote(z_send.at[peer], z_recv.at[chip], 6, 2 * peer + core, mr).start()

        return carry


    product = dot(d_pre, mean_mine, 0, 0)
    mean_copy.wait()
    dpre_copy.wait()

    across = math.isqrt(replicas)
    steps = sorted(
        ((dx, dy) for dx in range(across) for dy in range(across) if dx or dy),
        key=lambda step: (
            -sum(min(d, across - d) for d in step),
            min(step[0], across - step[0]) - min(step[1], across - step[1]),
        ),
    )

    def send_tiles(side):
        part = slice(side * lanes, (side + 1) * lanes)
        both = product[:, part] + dot(dpre_recv[...], mean_recv[:, part], 0, 0)
        tile_send[side] = both.astype(BF16).reshape(replicas, wide, lanes)
        tile_recv[side, mr] = tile_send[side, mr]

        for dx, dy in steps:
            peer = lax.rem(mr // across + dx, across) * across + lax.rem(mr + dy, across)
            remote(
                tile_send.at[side, peer], tile_recv.at[side, mr], 4 + side, mg, peer
            ).start()

    send_tiles(0)
    send_tiles(1)

    per = LANES // wide

    def plane_sum(side):
        wait_all(tile_recv.at[side], recv_sems.at[4 + side], replicas - 1)
        plane = tile_recv[side, 0].astype(F32)
        for p in range(1, replicas):
            plane = plane + tile_recv[side, p].astype(F32)
        if wide < LANES:
            plane = jnp.concatenate([plane, jnp.zeros((LANES - wide, lanes), F32)], axis=0)
        plane_t = plane.T
        for h in range(tall // per):
            packed = plane_t[h * per * wing : (h * per + 1) * wing, :]
            for i in range(1, per):
                e = h * per + i
                packed = packed + pltpu.roll(
                    plane_t[e * wing : (e + 1) * wing, :], i * wide, axis=1
                )
            for c in range(wing):
                z_send[side * wing + c, h : h + 1, :] = packed[c : c + 1, :]

    soon = 3 * groups // 16
    lax.fori_loop(0, soon, send_back, 0)
    total[...] = share.astype(F32) + dot(adj_t[:rows, :], share)
    plane_sum(0)
    lax.fori_loop(0, wing, send_z, 0)
    lax.fori_loop(soon, 2 * wing, send_back, 0)
    plane_sum(1)
    lax.fori_loop(wing, chips, send_z, 0)
    lax.fori_loop(2 * wing, groups, send_back, 0)
    z_recv[chip] = z_send[chip]

    wait_all(ret_recv, recv_sems.at[3], groups - 1)
    returned = unpack(ret_recv)
    d_rows = total[...]
    for k in range(capacity):
        d_rows = d_rows + dot(sent[k], returned[k * groups : (k + 1) * groups, :])
    row_out[...] = d_rows.astype(BF16)
    out_copy = pltpu.make_async_copy(row_out, d_features, load_sems.at[0])
    out_copy.start()

    wait_all(z_recv, recv_sems.at[6], chips - 1)
    block = jnp.sum(z_recv[...], axis=0) * (1.0 / math.sqrt(groups * replicas))
    for e in range(tall):
        line = block[e // per : e // per + 1, :]
        if e % per:
            line = pltpu.roll(line, LANES - (e % per) * wide, axis=1)
        weight_grad[e : e + 1, :] = line[:, :wide]

    wait_all(out_send, send_sems.at[7], 4 * near - 2)
    wait_all(out_send, send_sems.at[0], groups - 1)
    wait_all(ret_send, send_sems.at[3], groups - 1)
    out_copy.wait()
    wait_all(tile_send.at[0], send_sems.at[4], replicas - 1)
    wait_all(tile_send.at[1], send_sems.at[5], replicas - 1)
    wait_all(z_send, send_sems.at[6], chips - 1)


def hand_over(rows, block, rows_out, block_out):
    rows_out[...] = rows[...]
    block_out[...] = block[...]


def body(
    groups, replicas, features, neighbours, send_rows, send_counts, candidates, perturbation, weight
):
    rows, width = features.shape[1:]
    capacity = send_rows.shape[3]
    queries, cands = candidates.shape[1:]
    samples = perturbation.shape[2]
    slots = groups * capacity
    parts = capacity * width // LANES
    tall, wide = width // groups, width // replicas
    chips = groups // 2
    half = tall * chips
    packed = tall * wide // LANES
    args = (
        features[0],
        neighbours[0].T,
        send_rows[0, 0].T,
        send_counts[0],
        candidates[0],
        perturbation[0],
        weight,
    )
    vmem = pl.BlockSpec(memory_space=pltpu.VMEM)
    message = pltpu.VMEM((groups, parts, LANES), BF16)
    d_features, weight_grad = pl.pallas_call(
        functools.partial(kernel, groups, replicas),
        name="layer",
        out_shape=(
            jax.ShapeDtypeStruct((rows, width), BF16),
            jax.ShapeDtypeStruct((tall, wide), F32),
        ),
        in_specs=[pl.BlockSpec(memory_space=pl.ANY)] * 7,
        out_specs=(pl.BlockSpec(memory_space=pl.ANY), vmem),
        scratch_shapes=[pltpu.VMEM(x.shape, x.dtype) for x in args]
        + [
            pltpu.VMEM((groups * parts, LANES), F32),
            pltpu.VMEM((2 * groups, parts, LANES), BF16),
            message,
            pltpu.VMEM((2, chips // 2, parts, LANES), BF16),
            message,
            message,
            pltpu.VMEM((rows, half), BF16),
            pltpu.VMEM((rows, half), BF16),
            pltpu.VMEM((rows, width), BF16),
            pltpu.VMEM((rows, width), BF16),
            pltpu.VMEM((2, replicas, wide, half // 2), BF16),
            pltpu.VMEM((2, replicas, wide, half // 2), BF16),
            pltpu.VMEM((chips, packed, LANES), F32),
            pltpu.VMEM((chips, packed, LANES), F32),
            pltpu.VMEM((rows, rows + slots), BF16),
            pltpu.VMEM((rows + slots, rows), BF16),
            pltpu.VMEM((queries * rows, cands), BF16),
            pltpu.VMEM((samples, queries, cands), F32),
            pltpu.VMEM((rows, width), F32),
            pltpu.SemaphoreType.DMA((8,)),
            pltpu.SemaphoreType.DMA((8,)),
            pltpu.SemaphoreType.DMA((7,)),
            pltpu.SemaphoreType.DMA((2, chips // 4)),
            pltpu.VMEM((rows, width), BF16),
        ],
        compiler_params=pltpu.CompilerParams(
            collective_id=0, has_side_effects=True, vmem_limit_bytes=56 * 1024 * 1024
        ),
    )(*args)
    d_features, weight_grad = pl.pallas_call(
        hand_over,
        name="hand_over",
        out_shape=(
            jax.ShapeDtypeStruct((rows, width), BF16),
            jax.ShapeDtypeStruct((tall, wide), F32),
        ),
        in_specs=[vmem] * 2,
        out_specs=(vmem, vmem),
    )(d_features, weight_grad)
    return d_features[None], weight_grad


def solution(mesh):
    placed = (
        P("replica", "graph", None),
        P("replica", "graph", None),
        P("replica", "graph", None, None),
        P("replica", "graph", None),
        P("replica", "graph", None),
        P("replica", "graph", None, None),
        P(),
    )
    return jax.shard_map(
        functools.partial(body, mesh.shape["graph"], mesh.shape["replica"]),
        mesh=mesh,
        in_specs=placed,
        out_specs=(P("replica", "graph", None), P("graph", "replica")),
        check_vma=False,
    )
```
